32 devices in a mesh: ctx: 16 (over z, y, x), fsdp: 2 (over core).
Axes of the slice: x: 2, y: 2, z: 4, core: 2. Of those that a mesh axis runs over, the one named last changes fastest.
Arguments:
- tokens: bfloat16 [2, 2048, 768], P('fsdp', 'ctx'), may hold values from -6 to 6
- qkv_weight: bfloat16 [3, 768, 768], P(None, 'fsdp'), may hold values from -0.21875 to 0.21875
- out_weight: bfloat16 [768, 768], P('fsdp'), may hold values from -6 to 6
- bias_table: float32 [32, 12], replicated, may hold values from -4 to 4
- norm_gain: bfloat16 [2, 768], P(None, 'fsdp'), may hold values from 0.5 to 1.5
- router_weight: bfloat16 [768, 32], P('fsdp'), may hold values from -0.15625 to 0.15625
- expert_in: bfloat16 [32, 768, 3072], P('ctx', 'fsdp'), may hold values from -0.21875 to 0.21875
- expert_out: bfloat16 [32, 3072, 768], P('ctx', 'fsdp'), may hold values from -6 to 6
- expert_ids: int32 [2, 2048], P('fsdp', 'ctx'), may hold values from 0 to 31, as said below
- slot_ids: int32 [2, 2048], P('fsdp', 'ctx'), may hold values from 0 to 7, as said below
- bucket_table: int32 [4095], replicated, may hold values from 0 to 31, as said below
- grad_out: bfloat16 [2, 2048, 768], P('fsdp', 'ctx'), may hold values from -6 to 6
Outputs:
- layer_out: bfloat16 [2, 2048, 768], P('fsdp', 'ctx')
- grad_tokens: float32 [2, 2048, 768], P('fsdp', 'ctx')
- grad_qkv: float32 [3, 768, 768], P(None, 'fsdp')
- grad_out_weight: float32 [768, 768], P('fsdp')
- grad_bias: float32 [32, 12], P('fsdp')
- grad_gain: float32 [2, 768], P(None, 'fsdp')
- grad_router: float32 [768, 32], P('fsdp')
- grad_expert_in: float32 [32, 768, 3072], P('ctx', 'fsdp')
- grad_expert_out: float32 [32, 3072, 768], P('ctx', 'fsdp')
The draws below stay inside these ranges and needn't reach their ends.
Inputs may be any that keep to these rules, and one draw needn't show every extreme that they name: `expert_ids`: the tokens of one device name each expert at most 8 times, and some expert exactly 8 times. `slot_ids`: among one device's tokens, two that name the same expert never share a slot. `bucket_table`: entry 2047 + r holds the bucket of the offset r = key place - query place.
All inputs are finite; a program needn't handle non-finite values.
Results may differ from the reference program's by a relative error of at most 0.028.
Values may be sent and summed in bfloat16 or wider, within the bound.
A program may use at most 192 MiB of HBM per device.

```python
import math
import jax
import jax.numpy as jnp
from jax import lax

D = 768
HEADS = 12
HEAD_DIM = 64
FF = 3072
BUCKETS = 32
MAX_DIST = 128
TOK_DEV = 128
SEQ = 2048
SEQS = 2
EXPERTS = 32
CAP = 8
N_CTX = 16


def route_cells(key):
    cells = EXPERTS * CAP
    blocks = SEQS * N_CTX

    def one_block(block_key):
        favour_key, full_key, noise_key, order_key = jax.random.split(block_key, 4)
        owner = jnp.arange(cells, dtype=jnp.int32) // CAP
        favour = jax.random.randint(favour_key, (EXPERTS,), 0, 4)
        full_one = jax.random.randint(full_key, (), 0, EXPERTS)
        noise = jax.random.randint(noise_key, (cells,), 0, 65536)
        scores = jnp.where(owner == full_one, 0, favour[owner] * 65536 + noise + 1)
        scores = scores * cells + jnp.arange(cells, dtype=jnp.int32)
        picked = jnp.argsort(scores)[:TOK_DEV]
        picked = picked[jax.random.permutation(order_key, TOK_DEV)]
        return (picked // CAP, picked % CAP)
    owners, places = jax.vmap(one_block)(jax.random.split(key, blocks))
    return (owners.reshape(SEQS, SEQ).astype(jnp.int32), places.reshape(SEQS, SEQ).astype(jnp.int32))


def draw_expert_ids(key, part):
    return route_cells(key)[0]


def draw_slot_ids(key, part):
    return route_cells(key)[1]


def draw_bucket_table(key, part):
    key = jax.random.fold_in(key, 7)
    lower_key, upper_key = jax.random.split(key)
    half_count = BUCKETS // 2
    exact = half_count // 2
    spots = MAX_DIST - exact - 1

    def bounds(side_key):
        chosen = jax.random.permutation(side_key, spots)[:half_count - exact - 1] + exact + 1
        return jnp.sort(chosen)
    offsets = jnp.arange(2 * SEQ - 1, dtype=jnp.int32) - (SEQ - 1)
    distance = jnp.abs(offsets)

    def bucket_of(edges):
        counted = jnp.sum((distance[:, None] >= edges[None, :]).astype(jnp.int32), axis=1)
        return jnp.where(distance < exact, distance, exact + counted)
    result = jnp.where(offsets > 0, half_count + bucket_of(bounds(upper_key)), bucket_of(bounds(lower_key)))
    return result.astype(jnp.int32)


def steps_of(key, shape, cuts, least, largest):
    loudness, own = 1.0, jax.random.fold_in(key, 6)
    for axis_at, blocks in cuts:
        steps = jnp.exp(jax.random.uniform(jax.random.fold_in(own, axis_at), (blocks,), jnp.float32, least / len(cuts), largest / len(cuts)))
        loudness = loudness * jnp.repeat(steps, shape[axis_at] // blocks).reshape([-1 if axis == axis_at else 1 for axis in range(len(shape))])
    return loudness


def normal_values(rng, shape, spread, reach, cuts=(), held_as=jnp.bfloat16):
    values = spread * jax.random.normal(rng, shape, jnp.float32)
    if cuts:
        values = values * steps_of(rng, shape, cuts, -0.22, 0.18)
    return jnp.clip(values, -reach, reach).astype(held_as)


def setup_inputs(seed: int = 0) -> dict:
    arg_keys = jax.random.split(jax.random.key(seed), 13)
    tokens = normal_values(arg_keys[0], (SEQS, SEQ, D), 1.0, 6.0, ((0, 2), (1, 16)))
    qkv_weight = normal_values(arg_keys[1], (3, D, D), D ** -0.5, 0.21875, ((1, 2),))
    out_weight = normal_values(arg_keys[2], (D, D), 1.0, 6.0, ((0, 2),))
    bias_table = normal_values(arg_keys[3], (BUCKETS, HEADS), 1.0, 4.0, (), jnp.float32)
    norm_gain = jnp.clip(1.0 + 0.1 * jax.random.normal(arg_keys[4], (2, D), jnp.float32), 0.5, 1.5).astype(jnp.bfloat16)
    router_weight = normal_values(arg_keys[5], (D, EXPERTS), (2 * D) ** -0.5, 0.15625, ((0, 2),))
    expert_in = normal_values(arg_keys[6], (EXPERTS, D, FF), D ** -0.5, 0.21875, ((0, 16), (1, 2)))
    expert_out = normal_values(arg_keys[7], (EXPERTS, FF, D), (max(1, EXPERTS // 40)), 6.0, ((0, 16), (1, 2)))
    expert_ids = draw_expert_ids(jax.random.fold_in(arg_keys[12], 71), 0)
    slot_ids = draw_slot_ids(jax.random.fold_in(arg_keys[12], 71), 0)
    bucket_table = draw_bucket_table(jax.random.fold_in(arg_keys[12], 71), 0)
    grad_out = normal_values(arg_keys[11], (SEQS, SEQ, D), 1.0, 6.0, ((0, 2), (1, 16)))
    return dict(tokens=tokens, qkv_weight=qkv_weight, out_weight=out_weight, bias_table=bias_table, norm_gain=norm_gain, router_weight=router_weight, expert_in=expert_in, expert_out=expert_out, expert_ids=expert_ids, slot_ids=slot_ids, bucket_table=bucket_table, grad_out=grad_out)


epsilon = 1e-06
highest = lax.Precision.HIGHEST

@jax.custom_vjp
def low(v):
    return lax.optimization_barrier(v.astype(jnp.bfloat16)).astype(jnp.float32)

@jax.custom_vjp
def low_back(v):
    return v

def low_keep(v):
    return (low(v), None)

def low_pass(kept, grad):
    return (grad,)

def back_keep(v):
    return (v, None)

def back_low(kept, grad):
    return (low(grad),)
low.defvjp(low_keep, low_pass)
low_back.defvjp(back_keep, back_low)

def gelu_curve(values):
    return jax.nn.gelu(values, approximate=True)

def rms_apply(values, gain_vec):
    return values * lax.rsqrt(lax.optimization_barrier(jnp.mean(values * values, axis=-1, keepdims=True)) + epsilon) * gain_vec

def attention_sequence(query, key_rows, value_rows, bias_table, bucket_table):
    block_rows = math.gcd(SEQ, 1024)
    blocks = SEQ // block_rows
    key_heads = key_rows.reshape(SEQ, HEADS, HEAD_DIM)
    value_heads = value_rows.reshape(SEQ, HEADS, HEAD_DIM)
    places = jnp.arange(SEQ, dtype=jnp.int32)
    head_table = bias_table.T

    def one_block(block_args):
        query_block, first_row = block_args
        offset = places[None, :] - (first_row + jnp.arange(block_rows, dtype=jnp.int32))[:, None] + (SEQ - 1)
        pos_bias = jnp.take(head_table, jnp.take(bucket_table, offset), axis=1)
        scores = jnp.einsum('qhd,khd->hqk', query_block.reshape(block_rows, HEADS, HEAD_DIM), key_heads, precision=highest) * 0.125 + pos_bias
        weights = low(jax.nn.softmax(low_back(scores), axis=-1))
        mixed_rows = jnp.einsum('hqk,khd->qhd', weights, value_heads, precision=highest)
        return mixed_rows.reshape(block_rows, D)
    firsts = jnp.arange(blocks, dtype=jnp.int32) * block_rows
    mixed_rows = lax.map(jax.checkpoint(one_block), (query.reshape(blocks, block_rows, D), firsts))
    return mixed_rows.reshape(SEQ, D)

def expert_apply(expert_args):
    rows_in, weight_in, weight_out = expert_args
    pre_act = low_back(jnp.dot(rows_in, weight_in, precision=highest, preferred_element_type=jnp.float32))
    active = low(gelu_curve(pre_act))
    return low(low_back(jnp.dot(active, weight_out, precision=highest, preferred_element_type=jnp.float32)))

def layer_forward(tokens, qkv_weight, out_weight, bias_table, norm_gain, router_weight, expert_in, expert_out, expert_ids, slot_ids, bucket_table):
    total_rows = SEQS * SEQ
    residual = tokens.reshape(total_rows, D)
    normed = low(rms_apply(residual, norm_gain[0]))
    query = low(low_back(jnp.dot(normed, qkv_weight[0], precision=highest, preferred_element_type=jnp.float32)))
    key_rows = low(low_back(jnp.dot(normed, qkv_weight[1], precision=highest, preferred_element_type=jnp.float32)))
    value_rows = low(low_back(jnp.dot(normed, qkv_weight[2], precision=highest, preferred_element_type=jnp.float32)))

    def one_sequence(triple):
        return attention_sequence(triple[0], triple[1], triple[2], bias_table, bucket_table)
    shaped = (query.reshape(SEQS, SEQ, D), key_rows.reshape(SEQS, SEQ, D), value_rows.reshape(SEQS, SEQ, D))
    attended = lax.map(one_sequence, shaped).reshape(total_rows, D)
    attended = low(low_back(attended))
    middle = residual + low_back(jnp.dot(attended, out_weight, precision=highest, preferred_element_type=jnp.float32))
    second = low(rms_apply(middle, norm_gain[1]))
    router_prob = jax.nn.softmax(jnp.dot(second, router_weight, precision=highest, preferred_element_type=jnp.float32), axis=-1)
    owner = expert_ids.reshape(total_rows).astype(jnp.int32)
    chosen = (owner[:, None] == jnp.arange(EXPERTS, dtype=jnp.int32)[None, :]).astype(jnp.float32)
    gates = lax.optimization_barrier(jnp.sum(router_prob * chosen, axis=-1))
    column = jnp.arange(total_rows, dtype=jnp.int32) // TOK_DEV * CAP + slot_ids.reshape(total_rows).astype(jnp.int32)
    buffer = jnp.zeros((EXPERTS, total_rows // TOK_DEV * CAP, D), jnp.float32).at[owner, column].set(low_back(second))
    produced = lax.map(jax.checkpoint(expert_apply), (buffer, expert_in, expert_out))
    picked = produced[owner, column]
    return (middle + gates[:, None] * picked).reshape(SEQS, SEQ, D)

def reference(tokens, qkv_weight, out_weight, bias_table, norm_gain, router_weight, expert_in, expert_out, expert_ids, slot_ids, bucket_table, grad_out):
    floats = tuple((array.astype(jnp.float32) for array in (tokens, qkv_weight, out_weight, bias_table, norm_gain, router_weight, expert_in, expert_out)))

    def closed(*values):
        return layer_forward(*values, expert_ids, slot_ids, bucket_table)
    result, pullback = jax.vjp(closed, *floats)
    grads = pullback(grad_out.astype(jnp.float32))
    return (result.astype(jnp.bfloat16), grads[0], grads[1], grads[2], grads[3], grads[4], grads[5], grads[6], grads[7])
```

```python
import functools

import jax
import jax.numpy as jnp
from jax import lax
from jax.experimental import pallas as pl
from jax.experimental.pallas import tpu as pltpu
from jax.sharding import Mesh, PartitionSpec as P

HEADS = 12
GROUPS = 4
GROUP_HEADS = HEADS // GROUPS
SLAB = 128
Q_BLOCK = 128

epsilon = 1e-06


def gelu_curve(values):
    return jax.nn.gelu(values, approximate=True)


def rms_apply(values, gain_vec):
    factor = lax.rsqrt(jnp.mean(values * values, axis=-1, keepdims=True) + epsilon)
    return (values * factor * gain_vec, factor)


def rms_grad(values, factor, gain_vec, upstream):
    scaled = upstream * gain_vec
    inner_mean = jnp.mean(scaled * values, axis=-1, keepdims=True)
    return (
        factor * scaled - values * factor * factor * factor * inner_mean,
        jnp.sum(upstream * values * factor, axis=0),
    )


def dot_f32(a, b):
    return jnp.dot(a, b, preferred_element_type=jnp.float32)


def exact_dot(a, b):
    return jnp.dot(a, b, precision=lax.Precision.HIGHEST, preferred_element_type=jnp.float32)


def contract(a, b, dims):
    return lax.dot_general(a, b, (dims, ((), ())), preferred_element_type=jnp.float32)


def fill_toeplitz(line_ref, toeplitz):
    base = line_ref[0]
    for step in range(Q_BLOCK // 8):
        rows = base if step == 0 else pltpu.roll(base, 8 * step, 1)
        toeplitz[8 * step : 8 * step + 8, :] = rows


def forward_kernel(keys, blocks, q_ref, kv_ref, line_ref, out_ref, lse_ref, toeplitz):
    block = pl.program_id(1)

    @pl.when(block == 0)
    def _():
        fill_toeplitz(line_ref, toeplitz)

    start = pl.multiple_of((blocks - block) * Q_BLOCK, Q_BLOCK)
    slab = kv_ref[...]
    scores = contract(q_ref[...], slab, ((1,), (1,))) + toeplitz[:, pl.ds(start, keys)]
    top = jnp.max(scores, axis=-1, keepdims=True)
    weights = jnp.exp(scores - top)
    total = jnp.sum(weights, axis=-1, keepdims=True)
    mixed = dot_f32(weights.astype(jnp.bfloat16), slab)
    out_ref[...] = mixed / total
    lse_ref[0] = top + jnp.log(total)


def backward_kernel(
    keys,
    blocks,
    q_ref,
    kv_ref,
    line_ref,
    do_ref,
    out_ref,
    lse_ref,
    dq_ref,
    dkv_ref,
    diag_ref,
    toeplitz,
    folded,
    kv_sum,
):
    block = pl.program_id(1)

    @pl.when(block == 0)
    def _():
        fill_toeplitz(line_ref, toeplitz)
        folded[...] = jnp.zeros_like(folded)

    start = pl.multiple_of((blocks - block) * Q_BLOCK, Q_BLOCK)
    slab = kv_ref[...]
    queries = q_ref[...]
    upstream = do_ref[...]
    scores = contract(queries, slab, ((1,), (1,))) + toeplitz[:, pl.ds(start, keys)]
    probability = jnp.exp(scores - lse_ref[0])
    delta = jnp.sum(upstream.astype(jnp.float32) * out_ref[...], axis=-1, keepdims=True)
    score_grad = probability * (contract(upstream, slab, ((1,), (1,))) - delta)
    low = score_grad.astype(jnp.bfloat16)
    folded[:, pl.ds(start, keys)] += score_grad
    dq_ref[...] = (dot_f32(low, slab) * 0.125).astype(jnp.bfloat16)
    part = contract(low, queries, ((0,), (0,))) + contract(
        probability.astype(jnp.bfloat16), upstream, ((0,), (0,))
    )

    @pl.when(block == 0)
    def _():
        kv_sum[...] = part

    @pl.when(block > 0)
    def _():
        kv_sum[...] += part

    @pl.when(block == blocks - 1)
    def _():
        dkv_ref[...] = kv_sum[...].astype(jnp.bfloat16)
        grid = folded[...]
        width = grid.shape[1]
        half = Q_BLOCK // 2
        while half >= 8:
            grid = grid[:half] + pltpu.roll(grid[half:], width - half, 1)
            half //= 2
        diag_ref[0] = grid


def attention_specs(keys, width):
    return (
        pl.BlockSpec((Q_BLOCK, SLAB), lambda h, b: (b, h)),
        pl.BlockSpec((keys, SLAB), lambda h, b: (0, h)),
        pl.BlockSpec((1, 8, width), lambda h, b: (h, 0, 0)),
        pl.BlockSpec((1, Q_BLOCK, 1), lambda h, b: (h, b, 0)),
    )


def attend(q_slab, kv_slab, lines):
    rows, keys, width = q_slab.shape[0], kv_slab.shape[0], lines.shape[2]
    blocks = rows // Q_BLOCK
    q_spec, kv_spec, line_spec, lse_spec = attention_specs(keys, width)
    return pl.pallas_call(
        functools.partial(forward_kernel, keys, blocks),
        grid=(GROUP_HEADS, blocks),
        in_specs=[q_spec, kv_spec, line_spec],
        out_specs=[q_spec, lse_spec],
        out_shape=[
            jax.ShapeDtypeStruct(q_slab.shape, jnp.float32),
            jax.ShapeDtypeStruct((GROUP_HEADS, rows, 1), jnp.float32),
        ],
        scratch_shapes=[pltpu.VMEM((Q_BLOCK, width), jnp.float32)],
        compiler_params=pltpu.CompilerParams(vmem_limit_bytes=50 * 2**20),
        cost_estimate=pl.CostEstimate(
            flops=4 * rows * keys * SLAB * GROUP_HEADS,
            bytes_accessed=2 * (keys + 3 * rows) * SLAB * GROUP_HEADS,
            transcendentals=rows * keys * GROUP_HEADS,
        ),
        name="attend",
    )(q_slab, kv_slab, lines)


def attend_grad(q_slab, kv_slab, lines, do_slab, out_slab, lse):
    rows, keys, width = q_slab.shape[0], kv_slab.shape[0], lines.shape[2]
    blocks = rows // Q_BLOCK
    q_spec, kv_spec, line_spec, lse_spec = attention_specs(keys, width)
    return pl.pallas_call(
        functools.partial(backward_kernel, keys, blocks),
        grid=(GROUP_HEADS, blocks),
        in_specs=[q_spec, kv_spec, line_spec, q_spec, q_spec, lse_spec],
        out_specs=[q_spec, kv_spec, line_spec],
        out_shape=[
            jax.ShapeDtypeStruct(q_slab.shape, jnp.bfloat16),
            jax.ShapeDtypeStruct(kv_slab.shape, jnp.bfloat16),
            jax.ShapeDtypeStruct(lines.shape, jnp.float32),
        ],
        scratch_shapes=[
            pltpu.VMEM((Q_BLOCK, width), jnp.float32),
            pltpu.VMEM((Q_BLOCK, width), jnp.float32),
            pltpu.VMEM((keys, SLAB), jnp.float32),
        ],
        compiler_params=pltpu.CompilerParams(vmem_limit_bytes=58 * 2**20),
        cost_estimate=pl.CostEstimate(
            flops=10 * rows * keys * SLAB * GROUP_HEADS,
            bytes_accessed=4 * (keys + 3 * rows) * SLAB * GROUP_HEADS,
            transcendentals=rows * keys * GROUP_HEADS,
        ),
        name="attend_grad",
    )(q_slab, kv_slab, lines, do_slab, out_slab, lse)


def assemble_kernel(part_width, whole_ref, qkv_ref, out_ref):
    for matrix in range(4):
        first = matrix * part_width
        rows = jnp.concatenate(
            [
                whole_ref[g][:, first : first + part_width].astype(jnp.float32)
                for g in range(GROUPS)
            ],
            axis=1,
        )
        if matrix < 3:
            qkv_ref[matrix] = rows
        else:
            out_ref[...] = rows


def assemble(whole, part_width):
    row_count, columns = whole.shape[1], whole.shape[2]
    step = 96
    full = part_width * GROUPS
    return pl.pallas_call(
        functools.partial(assemble_kernel, part_width),
        grid=(row_count // step,),
        in_specs=[pl.BlockSpec((GROUPS, step, columns), lambda i: (0, i, 0))],
        out_specs=[
            pl.BlockSpec((3, step, full), lambda i: (0, i, 0)),
            pl.BlockSpec((step, full), lambda i: (i, 0)),
        ],
        out_shape=[
            jax.ShapeDtypeStruct((3, row_count, full), jnp.float32),
            jax.ShapeDtypeStruct((row_count, full), jnp.float32),
        ],
        name="assemble",
    )(whole)


def gather_rows(values, axis):
    return lax.all_gather(values, axis, axis=0, tiled=True)


def scatter_sum(values, axis_name, dim):
    if lax.axis_size(axis_name) != 2:
        return lax.psum_scatter(
            values.astype(jnp.bfloat16), axis_name, scatter_dimension=dim, tiled=True
        ).astype(jnp.float32)
    me = lax.axis_index(axis_name)
    half = values.shape[dim] // 2
    away = lax.dynamic_slice_in_dim(values, (1 - me) * half, half, dim).astype(jnp.bfloat16)
    kept = lax.dynamic_slice_in_dim(values, me * half, half, dim)
    other = lax.ppermute(away, axis_name, [(0, 1), (1, 0)])
    return kept + other.astype(jnp.float32)


def product_shard(left, right):
    if lax.axis_size("fsdp") != 2:
        return scatter_sum(
            jnp.einsum("eca,ecb->eab", left, right, preferred_element_type=jnp.float32), "fsdp", 1
        )
    me = lax.axis_index("fsdp")
    half = left.shape[2] // 2
    away, kept = (
        jnp.einsum(
            "eca,ecb->eab",
            lax.dynamic_slice_in_dim(left, which * half, half, 2),
            right,
            preferred_element_type=jnp.float32,
        )
        for which in (1 - me, me)
    )
    other = lax.ppermute(away.astype(jnp.bfloat16), "fsdp", [(0, 1), (1, 0)])
    return kept + other.astype(jnp.float32)


def per_device(
    tokens,
    qkv_weight,
    out_weight,
    bias_table,
    norm_gain,
    router_weight,
    expert_in,
    expert_out,
    expert_ids,
    slot_ids,
    bucket_table,
    grad_out,
):
    places_axes = ("z", "g")
    group = lax.axis_index("g")
    quarter = lax.axis_index("z")
    row_count = tokens.shape[1]
    model_width = tokens.shape[2]
    head_width = model_width // HEADS
    part_width = model_width // GROUPS
    quarter_rows = row_count * GROUPS
    key_count = quarter_rows * lax.axis_size("z")

    token_rows = tokens[0]
    quarter_tokens = gather_rows(token_rows, "g")
    own_columns = lax.dynamic_slice_in_dim(qkv_weight, group * part_width, part_width, 2)
    qkv_part = lax.all_gather(own_columns, "fsdp", axis=1, tiled=True)
    gain_full = lax.all_gather(norm_gain, "fsdp", axis=1, tiled=True)
    out_full = lax.all_gather(out_weight, "fsdp", axis=0, tiled=True)
    router_full = lax.all_gather(router_weight, "fsdp", axis=0, tiled=True)
    in_full = lax.all_gather(expert_in, "fsdp", axis=1, tiled=True)
    outer_full = lax.all_gather(expert_out, "fsdp", axis=1, tiled=True)

    expert_count = router_full.shape[1]
    capacity = max(2, 2 * row_count // expert_count)
    gains_float = gain_full.astype(jnp.float32)

    centre = (bucket_table.shape[0] - 1) // 2
    width = quarter_rows + key_count
    padded_table = jnp.pad(bucket_table, (1, 0))
    window = lax.dynamic_slice_in_dim(
        padded_table, centre + 1 - quarter_rows - quarter * quarter_rows, width, 0
    )
    bucket_count = bias_table.shape[0]
    marks = (jnp.arange(bucket_count, dtype=jnp.int32)[:, None] == window[None, :]).astype(
        jnp.float32
    )
    own_bias = lax.dynamic_slice_in_dim(bias_table, group * GROUP_HEADS, GROUP_HEADS, 1)
    line = exact_dot(own_bias.T, marks)
    lines = jnp.stack([jnp.roll(line, step, axis=1) for step in range(8)], axis=1)

    quarter_float = quarter_tokens.astype(jnp.float32)
    quarter_normed, quarter_factor = rms_apply(quarter_float, gains_float[0])
    quarter_normed = quarter_normed.astype(jnp.bfloat16)
    weight_heads = qkv_part.reshape(3, model_width, GROUP_HEADS, head_width)
    blank = jnp.zeros_like(weight_heads[0])
    slab_weight = jnp.stack(
        [
            jnp.concatenate([weight_heads[0], blank], axis=-1),
            jnp.concatenate([weight_heads[1], weight_heads[2]], axis=-1),
        ],
        axis=1,
    ).reshape(model_width, 2 * GROUP_HEADS * SLAB)
    projected = dot_f32(quarter_normed, slab_weight).astype(jnp.bfloat16)
    slab_columns = GROUP_HEADS * SLAB
    q_slab = projected[:, :slab_columns] * jnp.bfloat16(0.125)
    kv_slab = gather_rows(projected[:, slab_columns:], "z")
    out_slab, lse = attend(q_slab, kv_slab, lines)
    quarter_out = (
        out_slab.reshape(quarter_rows, GROUP_HEADS, SLAB)[:, :, head_width:]
        .reshape(quarter_rows, part_width)
        .astype(jnp.bfloat16)
    )
    mixed_low = lax.all_to_all(
        quarter_out.reshape(GROUPS, row_count, part_width), "g", 0, 0, tiled=True
    )
    mixed_low = jnp.transpose(mixed_low, (1, 0, 2)).reshape(row_count, model_width)
    quarter_mixed = gather_rows(mixed_low, "g")

    residual = token_rows.astype(jnp.float32)
    middle = residual + dot_f32(mixed_low, out_full)
    normed_two, factor_two = rms_apply(middle, gains_float[1])
    second_low = normed_two.astype(jnp.bfloat16)
    router_prob = jax.nn.softmax(dot_f32(second_low, router_full), axis=-1)
    owner = expert_ids[0]
    chosen = (owner[:, None] == jnp.arange(expert_count, dtype=jnp.int32)[None, :]).astype(
        jnp.float32
    )
    gates = jnp.sum(router_prob * chosen, axis=-1)
    upstream = grad_out[0].astype(jnp.float32)
    target = owner * capacity + slot_ids[0]
    pick = (target[:, None] == jnp.arange(expert_count * capacity, dtype=jnp.int32)).astype(
        jnp.bfloat16
    )

    both = jnp.concatenate([second_low, (gates[:, None] * upstream).astype(jnp.bfloat16)], axis=1)
    send_rows = contract(pick, both, ((0,), (0,))).astype(jnp.bfloat16)
    arrived = lax.all_to_all(send_rows, places_axes, 0, 0, tiled=True)
    place_count = lax.axis_size("z") * GROUPS
    local_count = expert_count // place_count

    def by_expert(rows):
        shaped = rows.reshape(place_count, local_count, capacity, rows.shape[1])
        return jnp.transpose(shaped, (1, 0, 2, 3)).reshape(
            local_count, place_count * capacity, rows.shape[1]
        )

    expert_rows = by_expert(arrived)
    rows_in = expert_rows[:, :, :model_width]
    rows_grad = expert_rows[:, :, model_width:]
    pre_act = jnp.einsum("ecd,edf->ecf", rows_in, in_full, preferred_element_type=jnp.float32)
    active, gelu_pull = jax.vjp(gelu_curve, pre_act)
    active_low = active.astype(jnp.bfloat16)
    produced = jnp.einsum(
        "ecf,efd->ecd", active_low, outer_full, preferred_element_type=jnp.float32
    ).astype(jnp.bfloat16)
    grad_active = jnp.einsum(
        "ecd,efd->ecf", rows_grad, outer_full, preferred_element_type=jnp.float32
    )
    grad_pre = gelu_pull(grad_active)[0].astype(jnp.bfloat16)
    grad_rows = jnp.einsum(
        "ecf,edf->ecd", grad_pre, in_full, preferred_element_type=jnp.float32
    ).astype(jnp.bfloat16)
    leaving = jnp.concatenate([produced, grad_rows], axis=2)
    leaving = jnp.transpose(
        leaving.reshape(local_count, place_count, capacity, 2 * model_width), (1, 0, 2, 3)
    ).reshape(expert_count * capacity, 2 * model_width)
    returned = lax.all_to_all(leaving, places_axes, 0, 0, tiled=True)
    final_outer = product_shard(active_low, rows_grad)
    final_inner = product_shard(rows_in, grad_pre)

    fetched = dot_f32(pick, returned)
    picked = fetched[:, :model_width]
    layer_out = (middle + gates[:, None] * picked).astype(jnp.bfloat16)
    gate_grad = jnp.sum(upstream * picked, axis=-1)
    logit_grad = router_prob * (chosen - gates[:, None]) * gate_grad[:, None]
    router_grad = exact_dot(second_low.astype(jnp.float32).T, logit_grad)
    grad_second = fetched[:, model_width:] + exact_dot(
        logit_grad, router_full.astype(jnp.float32).T
    )
    grad_middle, gain_two_grad = rms_grad(middle, factor_two, gains_float[1], grad_second)
    grad_middle = grad_middle + upstream
    quarter_middle = gather_rows(grad_middle.astype(jnp.bfloat16), "g")

    own_out = lax.dynamic_slice_in_dim(out_full, group * part_width, part_width, 0)
    own_out = own_out.reshape(GROUP_HEADS, head_width, model_width)
    own_out = jnp.concatenate([jnp.zeros_like(own_out), own_out], axis=1).reshape(
        slab_columns, model_width
    )
    do_slab = contract(quarter_middle, own_out, ((1,), (1,))).astype(jnp.bfloat16)
    dq_slab, dkv_part, diag = attend_grad(q_slab, kv_slab, lines, do_slab, out_slab, lse)
    diag_line = sum(jnp.roll(diag[:, step], -step, axis=1) for step in range(8))
    own_table = exact_dot(marks, diag_line.T)
    head_marks = (
        jnp.arange(HEADS, dtype=jnp.int32)[None, :]
        == (group * GROUP_HEADS + jnp.arange(GROUP_HEADS, dtype=jnp.int32))[:, None]
    ).astype(jnp.float32)
    grad_table = exact_dot(own_table, head_marks)
    dkv_parts = lax.all_to_all(dkv_part, "z", 0, 0, tiled=True)
    dkv = (
        jnp.sum(dkv_parts.reshape(-1, quarter_rows, slab_columns).astype(jnp.float32), axis=0)
        .astype(jnp.bfloat16)
    )

    def pick_half(slab, first):
        return slab.reshape(quarter_rows, GROUP_HEADS, SLAB)[
            :, :, first : first + head_width
        ].reshape(quarter_rows, part_width)

    grads_low = jnp.concatenate(
        [pick_half(dq_slab, 0), pick_half(dkv, 0), pick_half(dkv, head_width)], axis=1
    )
    qkv_columns = jnp.transpose(qkv_part, (1, 0, 2)).reshape(model_width, 3 * part_width)
    normed_part = contract(grads_low, qkv_columns, ((1,), (1,)))
    gain_one_part = jnp.sum(normed_part * quarter_float * quarter_factor, axis=0)
    normed_part = normed_part.astype(jnp.bfloat16)
    normed_parts = lax.all_to_all(
        normed_part.reshape(GROUPS, row_count, model_width), "g", 0, 0, tiled=True
    )
    grad_normed = jnp.sum(normed_parts.astype(jnp.float32), axis=0)
    factor_one = lax.rsqrt(jnp.mean(residual * residual, axis=-1, keepdims=True) + epsilon)
    grad_first, _ = rms_grad(residual, factor_one, gains_float[0], grad_normed)
    grad_tokens = (grad_first + grad_middle)[None]

    shard_count = lax.axis_size("fsdp")
    shard_rows = model_width // shard_count
    table_rows = bucket_count // shard_count
    table_column = jnp.pad(
        grad_table.reshape(shard_count, table_rows * HEADS),
        ((0, 0), (0, shard_rows - table_rows * HEADS)),
    ).reshape(model_width)
    small = jnp.concatenate(
        [
            router_grad,
            gain_one_part[:, None],
            gain_two_grad[:, None],
            table_column[:, None],
        ],
        axis=1,
    )
    small = jnp.pad(small, ((0, 0), (0, -small.shape[1] % 128)))
    own_middle = lax.dynamic_slice_in_dim(quarter_middle, group * part_width, part_width, 1)
    dense = jnp.concatenate(
        [
            contract(quarter_normed, grads_low, ((0,), (0,))),
            contract(quarter_mixed, own_middle, ((0,), (0,))),
            small,
        ],
        axis=1,
    )
    columns = dense.shape[1]
    dense = scatter_sum(dense, "fsdp", 0)
    quarter_count = lax.axis_size("z")
    pieces = lax.all_to_all(
        dense.astype(jnp.bfloat16).reshape(quarter_count, -1, columns), "z", 0, 0, tiled=True
    )
    summed = jnp.sum(pieces.astype(jnp.float32), axis=0).astype(jnp.bfloat16)
    whole = gather_rows(gather_rows(summed, "z"), "g").reshape(GROUPS, shard_rows, columns)
    final_qkv, final_out = assemble(whole, part_width)
    totals = jnp.sum(whole[:, :, model_width:].astype(jnp.float32), axis=0)
    table_total = totals[: table_rows * HEADS, expert_count + 2].reshape(table_rows, HEADS)
    return (
        layer_out[None],
        grad_tokens,
        final_qkv,
        final_out,
        table_total,
        totals[:, expert_count : expert_count + 2].T,
        totals[:, :expert_count],
        final_inner,
        final_outer,
    )


def solution(mesh):
    places = ("z", "g")
    devices = mesh.devices.reshape(mesh.shape["ctx"] // GROUPS, GROUPS, mesh.shape["fsdp"])
    finer = Mesh(devices, ("z", "g", "fsdp"))
    placed = (
        P("fsdp", places, None),
        P(None, "fsdp", None),
        P("fsdp", None),
        P(),
        P(None, "fsdp"),
        P("fsdp", None),
        P(places, "fsdp", None),
        P(places, "fsdp", None),
        P("fsdp", places),
        P("fsdp", places),
        P(),
        P("fsdp", places, None),
    )
    return jax.shard_map(
        per_device,
        mesh=finer,
        in_specs=placed,
        out_specs=(
            P("fsdp", places, None),
            P("fsdp", places, None),
            P(None, "fsdp", None),
            P("fsdp", None),
            P("fsdp", None),
            P(None, "fsdp"),
            P("fsdp", None),
            P(places, "fsdp", None),
            P(places, "fsdp", None),
        ),
        check_vma=False,
    )
```

```python
import functools

import jax
import jax.numpy as jnp
from jax import lax
from jax.experimental import pallas as pl
from jax.experimental.pallas import tpu as pltpu
from jax.sharding import Mesh, PartitionSpec as P

HEADS = 12
GROUPS = 4
GROUP_HEADS = HEADS // GROUPS
SLAB = 128
Q_BLOCK = 128

epsilon = 1e-06


def gelu_curve(values):
    return jax.nn.gelu(values, approximate=True)


def rms_apply(values, gain_vec):
    factor = lax.rsqrt(jnp.mean(values * values, axis=-1, keepdims=True) + epsilon)
    return (values * factor * gain_vec, factor)


def rms_grad(values, factor, gain_vec, upstream):
    scaled = upstream * gain_vec
    inner_mean = jnp.mean(scaled * values, axis=-1, keepdims=True)
    return (
        factor * scaled - values * factor * factor * factor * inner_mean,
        jnp.sum(upstream * values * factor, axis=0),
    )


def dot_f32(a, b):
    return jnp.dot(a, b, preferred_element_type=jnp.float32)


def exact_dot(a, b):
    return jnp.dot(a, b, precision=lax.Precision.HIGHEST, preferred_element_type=jnp.float32)


def contract(a, b, dims):
    return lax.dot_general(a, b, (dims, ((), ())), preferred_element_type=jnp.float32)


def fill_toeplitz(line_ref, toeplitz):
    base = line_ref[0]
    for step in range(Q_BLOCK // 8):
        rows = base if step == 0 else pltpu.roll(base, 8 * step, 1)
        toeplitz[8 * step : 8 * step + 8, :] = rows


def forward_kernel(keys, blocks, q_ref, kv_ref, line_ref, out_ref, lse_ref, toeplitz):
    block = pl.program_id(1)

    @pl.when(block == 0)
    def _():
        fill_toeplitz(line_ref, toeplitz)

    start = pl.multiple_of((blocks - block) * Q_BLOCK, Q_BLOCK)
    slab = kv_ref[...]
    scores = contract(q_ref[...], slab, ((1,), (1,))) + toeplitz[:, pl.ds(start, keys)]
    top = jnp.max(scores, axis=-1, keepdims=True)
    weights = jnp.exp(scores - top)
    total = jnp.sum(weights, axis=-1, keepdims=True)
    mixed = dot_f32(weights.astype(jnp.bfloat16), slab)
    out_ref[...] = mixed / total
    lse_ref[0] = top + jnp.log(total)


def backward_kernel(
    keys,
    blocks,
    q_ref,
    kv_ref,
    line_ref,
    do_ref,
    out_ref,
    lse_ref,
    dq_ref,
    dkv_ref,
    diag_ref,
    toeplitz,
    folded,
    kv_sum,
):
    block = pl.program_id(1)

    @pl.when(block == 0)
    def _():
        fill_toeplitz(line_ref, toeplitz)
        folded[...] = jnp.zeros_like(folded)

    start = pl.multiple_of((blocks - block) * Q_BLOCK, Q_BLOCK)
    slab = kv_ref[...]
    queries = q_ref[...]
    upstream = do_ref[...]
    scores = contract(queries, slab, ((1,), (1,))) + toeplitz[:, pl.ds(start, keys)]
    probability = jnp.exp(scores - lse_ref[0])
    delta = jnp.sum(upstream.astype(jnp.float32) * out_ref[...], axis=-1, keepdims=True)
    score_grad = probability * (contract(upstream, slab, ((1,), (1,))) - delta)
    low = score_grad.astype(jnp.bfloat16)
    folded[:, pl.ds(start, keys)] += score_grad
    dq_ref[...] = (dot_f32(low, slab) * 0.125).astype(jnp.bfloat16)
    part = contract(low, queries, ((0,), (0,))) + contract(
        probability.astype(jnp.bfloat16), upstream, ((0,), (0,))
    )

    @pl.when(block == 0)
    def _():
        kv_sum[...] = part

    @pl.when(block > 0)
    def _():
        kv_sum[...] += part

    @pl.when(block == blocks - 1)
    def _():
        dkv_ref[...] = kv_sum[...].astype(jnp.bfloat16)
        grid = folded[...]
        width = grid.shape[1]
        half = Q_BLOCK // 2
        while half >= 8:
            grid = grid[:half] + pltpu.roll(grid[half:], width - half, 1)
            half //= 2
        diag_ref[0] = grid


def attention_specs(keys, width):
    return (
        pl.BlockSpec((Q_BLOCK, SLAB), lambda h, b: (b, h)),
        pl.BlockSpec((keys, SLAB), lambda h, b: (0, h)),
        pl.BlockSpec((1, 8, width), lambda h, b: (h, 0, 0)),
        pl.BlockSpec((1, Q_BLOCK, 1), lambda h, b: (h, b, 0)),
    )


def attend(q_slab, kv_slab, lines):
    rows, keys, width = q_slab.shape[0], kv_slab.shape[0], lines.shape[2]
    blocks = rows // Q_BLOCK
    q_spec, kv_spec, line_spec, lse_spec = attention_specs(keys, width)
    return pl.pallas_call(
        functools.partial(forward_kernel, keys, blocks),
        grid=(GROUP_HEADS, blocks),
        in_specs=[q_spec, kv_spec, line_spec],
        out_specs=[q_spec, lse_spec],
        out_shape=[
            jax.ShapeDtypeStruct(q_slab.shape, jnp.float32),
            jax.ShapeDtypeStruct((GROUP_HEADS, rows, 1), jnp.float32),
        ],
        scratch_shapes=[pltpu.VMEM((Q_BLOCK, width), jnp.float32)],
        compiler_params=pltpu.CompilerParams(vmem_limit_bytes=50 * 2**20),
        cost_estimate=pl.CostEstimate(
            flops=4 * rows * keys * SLAB * GROUP_HEADS,
            bytes_accessed=2 * (keys + 3 * rows) * SLAB * GROUP_HEADS,
            transcendentals=rows * keys * GROUP_HEADS,
        ),
        name="attend",
    )(q_slab, kv_slab, lines)


def attend_grad(q_slab, kv_slab, lines, do_slab, out_slab, lse):
    rows, keys, width = q_slab.shape[0], kv_slab.shape[0], lines.shape[2]
    blocks = rows // Q_BLOCK
    q_spec, kv_spec, line_spec, lse_spec = attention_specs(keys, width)
    return pl.pallas_call(
        functools.partial(backward_kernel, keys, blocks),
        grid=(GROUP_HEADS, blocks),
        in_specs=[q_spec, kv_spec, line_spec, q_spec, q_spec, lse_spec],
        out_specs=[q_spec, kv_spec, line_spec],
        out_shape=[
            jax.ShapeDtypeStruct(q_slab.shape, jnp.bfloat16),
            jax.ShapeDtypeStruct(kv_slab.shape, jnp.bfloat16),
            jax.ShapeDtypeStruct(lines.shape, jnp.float32),
        ],
        scratch_shapes=[
            pltpu.VMEM((Q_BLOCK, width), jnp.float32),
            pltpu.VMEM((Q_BLOCK, width), jnp.float32),
            pltpu.VMEM((keys, SLAB), jnp.float32),
        ],
        compiler_params=pltpu.CompilerParams(vmem_limit_bytes=58 * 2**20),
        cost_estimate=pl.CostEstimate(
            flops=10 * rows * keys * SLAB * GROUP_HEADS,
            bytes_accessed=4 * (keys + 3 * rows) * SLAB * GROUP_HEADS,
            transcendentals=rows * keys * GROUP_HEADS,
        ),
        name="attend_grad",
    )(q_slab, kv_slab, lines, do_slab, out_slab, lse)


def assemble_kernel(part_width, whole_ref, qkv_ref, out_ref):
    for matrix in range(4):
        first = matrix * part_width
        rows = jnp.concatenate(
            [
                whole_ref[g][:, first : first + part_width].astype(jnp.float32)
                for g in range(GROUPS)
            ],
            axis=1,
        )
        if matrix < 3:
            qkv_ref[matrix] = rows
        else:
            out_ref[...] = rows


def assemble(whole, part_width):
    row_count, columns = whole.shape[1], whole.shape[2]
    step = 96
    full = part_width * GROUPS
    return pl.pallas_call(
        functools.partial(assemble_kernel, part_width),
        grid=(row_count // step,),
        in_specs=[pl.BlockSpec((GROUPS, step, columns), lambda i: (0, i, 0))],
        out_specs=[
            pl.BlockSpec((3, step, full), lambda i: (0, i, 0)),
            pl.BlockSpec((step, full), lambda i: (i, 0)),
        ],
        out_shape=[
            jax.ShapeDtypeStruct((3, row_count, full), jnp.float32),
            jax.ShapeDtypeStruct((row_count, full), jnp.float32),
        ],
        name="assemble",
    )(whole)


def gather_rows(values, axis):
    return lax.all_gather(values, axis, axis=0, tiled=True)


def scatter_sum(values, axis_name, dim):
    if lax.axis_size(axis_name) != 2:
        return lax.psum_scatter(
            values.astype(jnp.bfloat16), axis_name, scatter_dimension=dim, tiled=True
        ).astype(jnp.float32)
    me = lax.axis_index(axis_name)
    half = values.shape[dim] // 2
    away = lax.dynamic_slice_in_dim(values, (1 - me) * half, half, dim).astype(jnp.bfloat16)
    kept = lax.dynamic_slice_in_dim(values, me * half, half, dim)
    other = lax.ppermute(away, axis_name, [(0, 1), (1, 0)])
    return kept + other.astype(jnp.float32)


def product_rows(left, right, which):
    part = left.shape[2] // lax.axis_size("fsdp")
    return jnp.einsum(
        "eca,ecb->eab",
        lax.dynamic_slice_in_dim(left, which * part, part, 2),
        right,
        preferred_element_type=jnp.float32,
    )


def product_sum(left, right):
    return scatter_sum(
        jnp.einsum("eca,ecb->eab", left, right, preferred_element_type=jnp.float32), "fsdp", 1
    )


def per_device(
    tokens,
    qkv_weight,
    out_weight,
    bias_table,
    norm_gain,
    router_weight,
    expert_in,
    expert_out,
    expert_ids,
    slot_ids,
    bucket_table,
    grad_out,
):
    places_axes = ("z", "g")
    group = lax.axis_index("g")
    quarter = lax.axis_index("z")
    row_count = tokens.shape[1]
    model_width = tokens.shape[2]
    head_width = model_width // HEADS
    part_width = model_width // GROUPS
    quarter_rows = row_count * GROUPS
    key_count = quarter_rows * lax.axis_size("z")

    token_rows = tokens[0]
    quarter_tokens = gather_rows(token_rows, "g")
    own_columns = lax.dynamic_slice_in_dim(qkv_weight, group * part_width, part_width, 2)
    qkv_part = lax.all_gather(own_columns, "fsdp", axis=1, tiled=True)
    gain_full = lax.all_gather(norm_gain, "fsdp", axis=1, tiled=True)
    out_full = lax.all_gather(out_weight, "fsdp", axis=0, tiled=True)
    router_full = lax.all_gather(router_weight, "fsdp", axis=0, tiled=True)
    in_full = lax.all_gather(expert_in, "fsdp", axis=1, tiled=True)
    outer_full = lax.all_gather(expert_out, "fsdp", axis=1, tiled=True)

    expert_count = router_full.shape[1]
    capacity = max(2, 2 * row_count // expert_count)
    gains_float = gain_full.astype(jnp.float32)

    centre = (bucket_table.shape[0] - 1) // 2
    width = quarter_rows + key_count
    padded_table = jnp.pad(bucket_table, (1, 0))
    window = lax.dynamic_slice_in_dim(
        padded_table, centre + 1 - quarter_rows - quarter * quarter_rows, width, 0
    )
    bucket_count = bias_table.shape[0]
    marks = (jnp.arange(bucket_count, dtype=jnp.int32)[:, None] == window[None, :]).astype(
        jnp.float32
    )
    own_bias = lax.dynamic_slice_in_dim(bias_table, group * GROUP_HEADS, GROUP_HEADS, 1)
    line = exact_dot(own_bias.T, marks)
    lines = jnp.stack([jnp.roll(line, step, axis=1) for step in range(8)], axis=1)

    quarter_float = quarter_tokens.astype(jnp.float32)
    quarter_normed, quarter_factor = rms_apply(quarter_float, gains_float[0])
    quarter_normed = quarter_normed.astype(jnp.bfloat16)
    weight_heads = qkv_part.reshape(3, model_width, GROUP_HEADS, head_width)
    blank = jnp.zeros_like(weight_heads[0])
    slab_weight = jnp.stack(
        [
            jnp.concatenate([weight_heads[0], blank], axis=-1),
            jnp.concatenate([weight_heads[1], weight_heads[2]], axis=-1),
        ],
        axis=1,
    ).reshape(model_width, 2 * GROUP_HEADS * SLAB)
    projected = dot_f32(quarter_normed, slab_weight).astype(jnp.bfloat16)
    slab_columns = GROUP_HEADS * SLAB
    q_slab = projected[:, :slab_columns] * jnp.bfloat16(0.125)
    kv_slab = gather_rows(projected[:, slab_columns:], "z")
    out_slab, lse = attend(q_slab, kv_slab, lines)
    quarter_out = (
        out_slab.reshape(quarter_rows, GROUP_HEADS, SLAB)[:, :, head_width:]
        .reshape(quarter_rows, part_width)
        .astype(jnp.bfloat16)
    )
    quarter_mixed = jnp.transpose(lax.all_gather(quarter_out, "g", axis=0), (1, 0, 2)).reshape(
        quarter_rows, model_width
    )
    mixed_low = lax.dynamic_slice_in_dim(quarter_mixed, group * row_count, row_count, 0)

    residual = token_rows.astype(jnp.float32)
    middle = residual + dot_f32(mixed_low, out_full)
    normed_two, factor_two = rms_apply(middle, gains_float[1])
    second_low = normed_two.astype(jnp.bfloat16)
    router_prob = jax.nn.softmax(dot_f32(second_low, router_full), axis=-1)
    owner = expert_ids[0]
    chosen = (owner[:, None] == jnp.arange(expert_count, dtype=jnp.int32)[None, :]).astype(
        jnp.float32
    )
    gates = jnp.sum(router_prob * chosen, axis=-1)
    upstream = grad_out[0].astype(jnp.float32)
    target = owner * capacity + slot_ids[0]
    pick = (target[:, None] == jnp.arange(expert_count * capacity, dtype=jnp.int32)).astype(
        jnp.bfloat16
    )

    both = jnp.concatenate([second_low, (gates[:, None] * upstream).astype(jnp.bfloat16)], axis=1)
    send_rows = contract(pick, both, ((0,), (0,))).astype(jnp.bfloat16)
    arrived = lax.all_to_all(send_rows, places_axes, 0, 0, tiled=True)
    place_count = lax.axis_size("z") * GROUPS
    local_count = expert_count // place_count

    def by_expert(rows):
        shaped = rows.reshape(place_count, local_count, capacity, rows.shape[1])
        return jnp.transpose(shaped, (1, 0, 2, 3)).reshape(
            local_count, place_count * capacity, rows.shape[1]
        )

    expert_rows = by_expert(arrived)
    rows_in = expert_rows[:, :, :model_width]
    rows_grad = expert_rows[:, :, model_width:]
    pre_act = jnp.einsum("ecd,edf->ecf", rows_in, in_full, preferred_element_type=jnp.float32)
    active, gelu_pull = jax.vjp(gelu_curve, pre_act)
    active_low = active.astype(jnp.bfloat16)
    produced = jnp.einsum(
        "ecf,efd->ecd", active_low, outer_full, preferred_element_type=jnp.float32
    ).astype(jnp.bfloat16)
    grad_active = jnp.einsum(
        "ecd,efd->ecf", rows_grad, outer_full, preferred_element_type=jnp.float32
    )
    grad_pre = gelu_pull(grad_active)[0].astype(jnp.bfloat16)
    grad_rows = jnp.einsum(
        "ecf,edf->ecd", grad_pre, in_full, preferred_element_type=jnp.float32
    ).astype(jnp.bfloat16)
    leaving = jnp.concatenate([produced, grad_rows], axis=2)
    leaving = jnp.transpose(
        leaving.reshape(local_count, place_count, capacity, 2 * model_width), (1, 0, 2, 3)
    ).reshape(expert_count * capacity, 2 * model_width)
    returned = lax.all_to_all(leaving, places_axes, 0, 0, tiled=True)
    if lax.axis_size("fsdp") == 2:
        shard = lax.axis_index("fsdp")
        away_outer = product_rows(active_low, rows_grad, 1 - shard).astype(jnp.bfloat16)
        away_inner = product_rows(rows_in, grad_pre, 1 - shard).astype(jnp.bfloat16)
        returned, away_outer, away_inner = lax.optimization_barrier(
            (returned, away_outer, away_inner)
        )
        other_outer = lax.ppermute(away_outer, "fsdp", [(0, 1), (1, 0)]).astype(jnp.float32)
        other_inner = lax.ppermute(away_inner, "fsdp", [(0, 1), (1, 0)]).astype(jnp.float32)
        final_outer = product_rows(active_low, rows_grad, shard) + other_outer
        final_inner = product_rows(rows_in, grad_pre, shard) + other_inner
    else:
        final_outer = product_sum(active_low, rows_grad)
        final_inner = product_sum(rows_in, grad_pre)

    fetched = dot_f32(pick, returned)
    picked = fetched[:, :model_width]
    layer_out = (middle + gates[:, None] * picked).astype(jnp.bfloat16)
    gate_grad = jnp.sum(upstream * picked, axis=-1)
    logit_grad = router_prob * (chosen - gates[:, None]) * gate_grad[:, None]
    router_grad = exact_dot(second_low.astype(jnp.float32).T, logit_grad)
    grad_second = fetched[:, model_width:] + exact_dot(
        logit_grad, router_full.astype(jnp.float32).T
    )
    grad_middle, gain_two_grad = rms_grad(middle, factor_two, gains_float[1], grad_second)
    grad_middle = grad_middle + upstream
    quarter_middle = gather_rows(grad_middle.astype(jnp.bfloat16), "g")

    own_out = lax.dynamic_slice_in_dim(out_full, group * part_width, part_width, 0)
    own_out = own_out.reshape(GROUP_HEADS, head_width, model_width)
    own_out = jnp.concatenate([jnp.zeros_like(own_out), own_out], axis=1).reshape(
        slab_columns, model_width
    )
    do_slab = contract(quarter_middle, own_out, ((1,), (1,))).astype(jnp.bfloat16)
    dq_slab, dkv_part, diag = attend_grad(q_slab, kv_slab, lines, do_slab, out_slab, lse)
    diag_line = sum(jnp.roll(diag[:, step], -step, axis=1) for step in range(8))
    own_table = exact_dot(marks, diag_line.T)
    head_marks = (
        jnp.arange(HEADS, dtype=jnp.int32)[None, :]
        == (group * GROUP_HEADS + jnp.arange(GROUP_HEADS, dtype=jnp.int32))[:, None]
    ).astype(jnp.float32)
    grad_table = exact_dot(own_table, head_marks)
    dkv_parts = lax.all_to_all(dkv_part, "z", 0, 0, tiled=True)
    dkv = (
        jnp.sum(dkv_parts.reshape(-1, quarter_rows, slab_columns).astype(jnp.float32), axis=0)
        .astype(jnp.bfloat16)
    )

    def pick_half(slab, first):
        return slab.reshape(quarter_rows, GROUP_HEADS, SLAB)[
            :, :, first : first + head_width
        ].reshape(quarter_rows, part_width)

    grads_low = jnp.concatenate(
        [pick_half(dq_slab, 0), pick_half(dkv, 0), pick_half(dkv, head_width)], axis=1
    )
    qkv_columns = jnp.transpose(qkv_part, (1, 0, 2)).reshape(model_width, 3 * part_width)
    normed_part = contract(grads_low, qkv_columns, ((1,), (1,)))
    gain_one_part = jnp.sum(normed_part * quarter_float * quarter_factor, axis=0)
    normed_part = normed_part.astype(jnp.bfloat16)
    normed_parts = lax.all_to_all(
        normed_part.reshape(GROUPS, row_count, model_width), "g", 0, 0, tiled=True
    )
    grad_normed = jnp.sum(normed_parts.astype(jnp.float32), axis=0)
    factor_one = lax.rsqrt(jnp.mean(residual * residual, axis=-1, keepdims=True) + epsilon)
    grad_first, _ = rms_grad(residual, factor_one, gains_float[0], grad_normed)
    grad_tokens = (grad_first + grad_middle)[None]

    shard_count = lax.axis_size("fsdp")
    shard_rows = model_width // shard_count
    table_rows = bucket_count // shard_count
    table_column = jnp.pad(
        grad_table.reshape(shard_count, table_rows * HEADS),
        ((0, 0), (0, shard_rows - table_rows * HEADS)),
    ).reshape(model_width)
    small = jnp.concatenate(
        [
            router_grad,
            gain_one_part[:, None],
            gain_two_grad[:, None],
            table_column[:, None],
        ],
        axis=1,
    )
    small = jnp.pad(small, ((0, 0), (0, -small.shape[1] % 128)))
    own_middle = lax.dynamic_slice_in_dim(quarter_middle, group * part_width, part_width, 1)
    dense = jnp.concatenate(
        [
            contract(quarter_normed, grads_low, ((0,), (0,))),
            contract(quarter_mixed, own_middle, ((0,), (0,))),
            small,
        ],
        axis=1,
    )
    columns = dense.shape[1]
    dense = scatter_sum(dense, "fsdp", 0)
    quarter_count = lax.axis_size("z")
    pieces = lax.all_to_all(
        dense.astype(jnp.bfloat16).reshape(quarter_count, -1, columns), "z", 0, 0, tiled=True
    )
    summed = jnp.sum(pieces.astype(jnp.float32), axis=0).astype(jnp.bfloat16)
    whole = gather_rows(gather_rows(summed, "z"), "g").reshape(GROUPS, shard_rows, columns)
    final_qkv, final_out = assemble(whole, part_width)
    totals = jnp.sum(whole[:, :, model_width:].astype(jnp.float32), axis=0)
    table_total = totals[: table_rows * HEADS, expert_count + 2].reshape(table_rows, HEADS)
    return (
        layer_out[None],
        grad_tokens,
        final_qkv,
        final_out,
        table_total,
        totals[:, expert_count : expert_count + 2].T,
        totals[:, :expert_count],
        final_inner,
        final_outer,
    )


def solution(mesh):
    places = ("z", "g")
    devices = mesh.devices.reshape(mesh.shape["ctx"] // GROUPS, GROUPS, mesh.shape["fsdp"])
    finer = Mesh(devices, ("z", "g", "fsdp"))
    placed = (
        P("fsdp", places, None),
        P(None, "fsdp", None),
        P("fsdp", None),
        P(),
        P(None, "fsdp"),
        P("fsdp", None),
        P(places, "fsdp", None),
        P(places, "fsdp", None),
        P("fsdp", places),
        P("fsdp", places),
        P(),
        P("fsdp", places, None),
    )
    return jax.shard_map(
        per_device,
        mesh=finer,
        in_specs=placed,
        out_specs=(
            P("fsdp", places, None),
            P("fsdp", places, None),
            P(None, "fsdp", None),
            P("fsdp", None),
            P("fsdp", None),
            P(None, "fsdp"),
            P("fsdp", None),
            P(places, "fsdp", None),
            P(places, "fsdp", None),
        ),
        check_vma=False,
    )
```
